32 devices in a mesh: rows: 4 (over y, x), ctx: 8 (over z, core).
Axes of the slice: x: 2, y: 2, z: 4, core: 2. Of those that a mesh axis runs over, the one named last changes fastest.
Arguments:
- queries: bfloat16 [512, 4096], P('rows'), may hold values from -15 to 15
- prefix_key_cache: bfloat16 [8192, 512], P('ctx'), may hold values from -24 to 24
- prefix_value_cache: bfloat16 [8192, 512], P('ctx'), may hold values from -6 to 6
- fresh_token_key: bfloat16 [512, 512], P('rows'), may hold values from -9 to 9
- fresh_token_value: bfloat16 [512, 512], P('rows'), may hold values from -6 to 6
- w_out: bfloat16 [4096, 2048], P('ctx'), may hold values from -0.09375 to 0.09375
- resid_in: bfloat16 [512, 2048], P(('rows', 'ctx')), may hold values from -1.5 to 1.5
- norm_gain: float32 [2048], replicated, may hold values from 0.3 to 3
- expert_ids: int32 [512, 8], P(('rows', 'ctx')), may hold values from 0 to 31, all different within a row; in each aligned block of 16 rows (0 to 15, 16 to 31, ...) at most 6 rows name the same one
- route_weight: float32 [512, 8], P(('rows', 'ctx')), may hold values from 0.05 to 0.5
- expert_place: int32 [32], replicated, may hold values from 0 to 31, each once
- w_gate: bfloat16 [32, 2048, 768], P(('rows', 'ctx')), may hold values from -0.125 to 0.125
- w_up: bfloat16 [32, 2048, 768], P(('rows', 'ctx')), may hold values from -0.125 to 0.125
- w_down: bfloat16 [32, 768, 2048], P(('rows', 'ctx')), may hold values from -0.21875 to 0.21875
Outputs:
- layer_out: bfloat16 [512, 2048], P(('rows', 'ctx'))
The draws below stay inside these ranges and needn't reach their ends.
Inputs may be any that keep to these rules, and one draw needn't show every extreme that they name: `expert_ids`: the 8 experts of a row differ. In the rows of one device (aligned blocks of 16 rows) no expert is named by more than 6 rows, a bound that some block reaches. `expert_place`: each slot holds exactly one expert.
All inputs are finite; a program needn't handle non-finite values.
Results may differ from the reference program's by a relative error of at most 0.02.
Values may be sent and summed in bfloat16 or wider, within the bound.
A program may use at most 192 MiB of HBM per device.

```python
import math
import jax
import jax.numpy as jnp
import numpy as np
from jax import lax

D = 2048
QUERY_HEADS = 32
KEY_HEADS = 4
HEAD_WIDTH = 128
FF = 768
TOP = 8
R_DEV = 128
SAMPLED_ROWS = 512
PREFIX_LENGTH = 8192
EXPERTS = 32
CAP = 6
N_ROWS = 4
N_CTX = 8


def draw_queries(key, part):
    random_seed_key = jax.random.fold_in(key, 11)
    return jnp.clip(2.5 * jax.random.normal(random_seed_key, (SAMPLED_ROWS, QUERY_HEADS * HEAD_WIDTH), jnp.float32), -15.0, 15.0).astype(jnp.bfloat16)


def draw_prefix_key_cache(key, part):
    random_seed_key = jax.random.fold_in(key, 12)
    return jnp.clip(jax.random.normal(random_seed_key, (PREFIX_LENGTH, KEY_HEADS * HEAD_WIDTH), jnp.float32), -5.0, 5.0).astype(jnp.bfloat16)


def shard_levels(own_key, dims, cuts, least, top_value):
    loudness = 1.0
    for dim, blocks in cuts:
        draws = jax.random.uniform(jax.random.fold_in(jax.random.fold_in(own_key, 6), dim), (blocks,), jnp.float32, least / len(cuts), top_value / len(cuts))
        loudness = loudness * jnp.repeat(jnp.exp(draws), dims[dim] // blocks).reshape((-1,) + (1,) * (len(dims) - 1 - dim))
    return loudness


def deal_out(own_key, own, number, rows, number_of, top, reach, slope):
    ranking = jax.random.permutation(own_key, number_of)
    packed, usual = shares(number_of, rows * top, reach, slope, True), shares(number_of, rows * top, reach, slope, False)
    places = jnp.arange(number_of)

    def named(tallies, turn):
        used = int((tallies > 0).sum())
        fixed = max(1, used // 4)
        moved = fixed + (places - fixed + turn * (used - fixed)) % max(1, number_of - fixed)
        return jnp.zeros((number_of,), jnp.int32).at[ranking[jnp.where(places < fixed, places, moved)]].set(jnp.asarray(tallies, jnp.int32))

    tallies = jnp.where(number % 4 == 0, named(packed, number // 4), named(usual, number - number // 4 - 1))
    mixed = jax.random.permutation(jax.random.fold_in(own, 3), number_of)
    donor, taker = mixed[0:number_of // 2 * 2:2], mixed[1:number_of // 2 * 2:2]
    margin = jnp.minimum(tallies[donor] - 1, reach - tallies[taker]) // 2
    margin = jnp.where((donor == ranking[0]) | (taker == ranking[0]) | (tallies[taker] == 0), 0, jnp.maximum(margin, 0))
    moved = jax.random.randint(jax.random.fold_in(own, 4), (number_of // 2,), 0, 1 << 20) % (margin + 1)
    tallies = tallies.at[donor].add(-moved).at[taker].add(moved)
    members = jnp.searchsorted(jnp.cumsum(tallies), jnp.arange(rows * top), side="right").astype(jnp.int32)
    grid = members.reshape(top, rows).T
    grid = grid[jax.random.permutation(jax.random.fold_in(own, 1), rows)]
    turn = jax.random.randint(jax.random.fold_in(own, 2), (rows, 1), 0, top)
    return jnp.take_along_axis(grid, (jnp.arange(top)[None, :] + turn) % top, axis=1)


def shares(number_of, total, limit, slope, full):
    portions = [(1 << 20) // math.isqrt(rank ** slope) + 1 for rank in range(1, number_of + 1)]
    largest = limit if full else min(limit, max(-(-total // number_of), total * portions[0] // sum(portions)))
    least = 1 if total - largest >= number_of - 1 else 0
    holding, rest = [largest] + [least] * (number_of - 1), total - largest - least * (number_of - 1)
    while rest > 0:
        candidates = [i for i in range(1, number_of) if holding[i] < largest] or [i for i in range(1, number_of) if holding[i] < limit]
        whole, budget = sum([portions[i] for i in candidates]), rest
        for i in candidates:
            extra = min(limit - holding[i], max(1, budget * portions[i] // whole), rest)
            holding[i] = holding[i] + extra
            rest = rest - extra
    return np.array(holding)


def centred(own_key, shape, deviation, bound, pieces=(), kind=jnp.bfloat16):
    gain = shard_levels(own_key, shape, pieces, -0.22, 0.18) if pieces else 1.0
    values = jax.random.normal(own_key, shape, jnp.float32) * deviation * gain
    return jnp.minimum(jnp.maximum(values, -bound), bound).astype(kind)


def setup_inputs(seed: int = 0) -> dict:
    seeds = jax.random.split(jax.random.key(seed), 15)
    queries = draw_queries(jax.random.fold_in(seeds[14], 71), 0)
    prefix_key_cache = draw_prefix_key_cache(jax.random.fold_in(seeds[14], 71), 0)
    prefix_value_cache = centred(seeds[2], (PREFIX_LENGTH, KEY_HEADS * HEAD_WIDTH), 1.0, 6.0, ((0, 8),))
    fresh_token_key = centred(seeds[3], (SAMPLED_ROWS, KEY_HEADS * HEAD_WIDTH), 1.5, 9.0, ((0, 4),))
    fresh_token_value = centred(seeds[4], (SAMPLED_ROWS, KEY_HEADS * HEAD_WIDTH), 1.0, 6.0, ((0, 4),))
    w_out = centred(seeds[5], (QUERY_HEADS * HEAD_WIDTH, D), (QUERY_HEADS * HEAD_WIDTH) ** -0.5, 0.09375, ((0, 8),))
    resid_in = centred(seeds[6], (SAMPLED_ROWS, D), 0.25, 1.5, ((0, 32),))
    norm_gain = jnp.clip(jnp.exp(jax.random.uniform(seeds[7], (D,), jnp.float32, math.log(0.3), math.log(3.0))), 0.3, 3.0)
    expert_ids_keys = jax.random.split(jax.random.fold_in(seeds[8], 1), SAMPLED_ROWS // (R_DEV // N_CTX))
    expert_ids_turns = jax.random.permutation(jax.random.fold_in(seeds[8], 3), SAMPLED_ROWS // (R_DEV // N_CTX))
    expert_ids = jax.vmap(lambda own, number: deal_out(jax.random.fold_in(seeds[8], 2), own, number, R_DEV // N_CTX, EXPERTS, TOP, CAP, 2))(expert_ids_keys, expert_ids_turns).reshape((SAMPLED_ROWS, TOP))
    route_weight = jnp.clip(0.05 + 0.45 * jax.random.uniform(seeds[9], (SAMPLED_ROWS, TOP), jnp.float32) ** shard_levels(seeds[9], (SAMPLED_ROWS, TOP), ((0, 32),), -0.2, 0.2), 0.05, 0.5)
    expert_place = jax.random.permutation(seeds[10], EXPERTS).astype(jnp.int32)
    w_gate = centred(seeds[11], (EXPERTS, D, FF), D ** -0.5, 0.125, ((0, 32),))
    w_up = centred(seeds[12], (EXPERTS, D, FF), D ** -0.5, 0.125, ((0, 32),))
    w_down = centred(seeds[13], (EXPERTS, FF, D), FF ** -0.5, 0.21875, ((0, 32),))
    return dict(queries=queries, prefix_key_cache=prefix_key_cache, prefix_value_cache=prefix_value_cache, fresh_token_key=fresh_token_key, fresh_token_value=fresh_token_value, w_out=w_out, resid_in=resid_in, norm_gain=norm_gain, expert_ids=expert_ids, route_weight=route_weight, expert_place=expert_place, w_gate=w_gate, w_up=w_up, w_down=w_down)


def reference(queries, prefix_key_cache, prefix_value_cache, fresh_token_key, fresh_token_value, w_out, resid_in, norm_gain, expert_ids, route_weight, expert_place, w_gate, w_up, w_down):
    query_group_width = QUERY_HEADS // KEY_HEADS
    score_scale = 1.0 / math.sqrt(HEAD_WIDTH)
    prefix_keys = prefix_key_cache.astype(jnp.float32).reshape(PREFIX_LENGTH, KEY_HEADS, HEAD_WIDTH)
    prefix_values = prefix_value_cache.astype(jnp.float32).reshape(PREFIX_LENGTH, KEY_HEADS, HEAD_WIDTH)
    row_tile = 32

    def attend(block_index):
        start_position = block_index * row_tile
        query_tile = lax.dynamic_slice_in_dim(queries, start_position, row_tile, 0).astype(jnp.float32).reshape(row_tile, KEY_HEADS, query_group_width, HEAD_WIDTH)
        fresh_keys = lax.dynamic_slice_in_dim(fresh_token_key, start_position, row_tile, 0).astype(jnp.float32).reshape(row_tile, KEY_HEADS, HEAD_WIDTH)
        fresh_values = lax.dynamic_slice_in_dim(fresh_token_value, start_position, row_tile, 0).astype(jnp.float32).reshape(row_tile, KEY_HEADS, HEAD_WIDTH)
        scores = jnp.einsum('bhgd,khd->bhgk', query_tile, prefix_keys) * score_scale
        own_score = jnp.einsum('bhgd,bhd->bhg', query_tile, fresh_keys) * score_scale
        maxima = jnp.maximum(lax.optimization_barrier(jnp.max(scores, -1)), own_score)
        weights = jnp.exp(scores - maxima[..., None])
        own_weight = jnp.exp(own_score - maxima)
        rounded = lax.optimization_barrier(weights.astype(jnp.bfloat16)).astype(jnp.float32)
        numer = jnp.einsum('bhgk,khd->bhgd', rounded, prefix_values) + own_weight[..., None] * fresh_values[:, :, None, :]
        denom = lax.optimization_barrier(jnp.sum(weights, -1)) + own_weight
        return (numer / denom[..., None]).reshape(row_tile, QUERY_HEADS * HEAD_WIDTH).astype(jnp.bfloat16)
    attention = lax.map(attend, jnp.arange(SAMPLED_ROWS // row_tile, dtype=jnp.int32)).reshape(SAMPLED_ROWS, QUERY_HEADS * HEAD_WIDTH)
    residual = (resid_in.astype(jnp.float32) + jnp.dot(attention, w_out, preferred_element_type=jnp.float32)).astype(jnp.bfloat16)
    widened = residual.astype(jnp.float32)
    normed = (widened * lax.rsqrt(lax.optimization_barrier(jnp.mean(widened * widened, -1, keepdims=True)) + 1e-06) * norm_gain).astype(jnp.bfloat16)
    expert_cap = CAP * N_ROWS * N_CTX

    def one_expert(running, expert):
        match_mask = expert_ids == expert
        chosen = jnp.any(match_mask, 1)
        weight = lax.optimization_barrier(jnp.sum(jnp.where(match_mask, route_weight, 0.0), 1))
        picked = jnp.argsort(1 - chosen.astype(jnp.int32), stable=True)[:expert_cap]
        stored = expert_place[expert]
        inputs = normed[picked]
        gate_proj = jnp.dot(inputs, w_gate[stored], preferred_element_type=jnp.float32)
        up_proj = jnp.dot(inputs, w_up[stored], preferred_element_type=jnp.float32)
        activated = (jax.nn.silu(gate_proj) * up_proj).astype(jnp.bfloat16)
        expert_out = jnp.dot(activated, w_down[stored], preferred_element_type=jnp.float32)
        expert_out = lax.optimization_barrier(expert_out.astype(jnp.bfloat16)).astype(jnp.float32)
        running = running.at[picked].add(expert_out * weight[picked][:, None])
        return (running, None)
    expert_sum, _ = lax.scan(one_expert, jnp.zeros((SAMPLED_ROWS, D), jnp.float32), jnp.arange(EXPERTS, dtype=jnp.int32))
    return (widened + expert_sum).astype(jnp.bfloat16)
```

```python
import math

import jax
import jax.numpy as jnp
from jax import lax
from jax.sharding import PartitionSpec as P

D = 2048
QUERY_HEADS = 32
KEY_HEADS = 4
HEAD_WIDTH = 128
TOP = 8


def run_experts(arrived, w_gate, w_up, w_down):
    gate_proj = jnp.einsum("sjcd,jdf->sjcf", arrived, w_gate, preferred_element_type=jnp.float32)
    up_proj = jnp.einsum("sjcd,jdf->sjcf", arrived, w_up, preferred_element_type=jnp.float32)
    activated = (jax.nn.silu(gate_proj) * up_proj).astype(jnp.bfloat16)
    produced = jnp.einsum("sjcf,jfd->sjcd", activated, w_down, preferred_element_type=jnp.float32)
    return produced.astype(jnp.bfloat16)


def shards(
    queries,
    prefix_key_cache,
    prefix_value_cache,
    fresh_token_key,
    fresh_token_value,
    w_out,
    resid_in,
    norm_gain,
    expert_ids,
    route_weight,
    expert_place,
    w_gate,
    w_up,
    w_down,
):
    rows_here = queries.shape[0]
    prefix_local = prefix_key_cache.shape[0]
    ctx_count = lax.axis_size("ctx")
    group_count = lax.axis_size("rows")
    ctx_index = lax.axis_index("ctx")
    query_group_width = QUERY_HEADS // KEY_HEADS
    score_scale = 1.0 / math.sqrt(HEAD_WIDTH)
    prefix_keys = prefix_key_cache.reshape(prefix_local, KEY_HEADS, HEAD_WIDTH)
    prefix_values = prefix_value_cache.reshape(prefix_local, KEY_HEADS, HEAD_WIDTH)
    is_first = ctx_index == 0
    row_tile = min(rows_here, 128)

    def partial_block(block_index):
        query_tile = queries.reshape(row_tile, KEY_HEADS, query_group_width, HEAD_WIDTH)
        fresh_keys = fresh_token_key.reshape(row_tile, KEY_HEADS, HEAD_WIDTH)
        fresh_values = fresh_token_value.reshape(row_tile, KEY_HEADS, HEAD_WIDTH)
        scores = (
            jnp.einsum(
                "bhgd,khd->bhgk", query_tile, prefix_keys, preferred_element_type=jnp.float32
            )
            * score_scale
        )
        own_score = (
            jnp.einsum("bhgd,bhd->bhg", query_tile, fresh_keys, preferred_element_type=jnp.float32)
            * score_scale
        )
        own_score = jnp.where(is_first, own_score, -1e30)
        maxima = jnp.maximum(jnp.max(scores, -1), own_score)
        weights = jnp.exp(scores - maxima[..., None])
        own_weight = jnp.exp(own_score - maxima)
        accum = jnp.einsum(
            "bhgk,khd->bhgd",
            weights.astype(jnp.bfloat16),
            prefix_values,
            preferred_element_type=jnp.float32,
        )
        accum = accum + own_weight[..., None] * fresh_values.astype(jnp.float32)[:, :, None, :]
        totals = jnp.sum(weights, -1) + own_weight
        return (
            maxima.reshape(row_tile, QUERY_HEADS),
            totals.reshape(row_tile, QUERY_HEADS),
            accum.reshape(row_tile, QUERY_HEADS, HEAD_WIDTH),
        )

    maxima, totals, accum = lax.map(
        partial_block, jnp.arange(rows_here // row_tile, dtype=jnp.int32)
    )
    maxima = maxima.reshape(rows_here, QUERY_HEADS)
    totals = totals.reshape(rows_here, QUERY_HEADS)
    accum = accum.reshape(rows_here, QUERY_HEADS, HEAD_WIDTH)
    heads_local = QUERY_HEADS // ctx_count
    global_max = lax.pmax(maxima, "ctx")
    factor = jnp.exp(maxima - global_max)
    accum_mine, totals_mine = (
        lax.psum_scatter(accum * factor[..., None], "ctx", scatter_dimension=1, tiled=True),
        lax.psum_scatter(totals * factor, "ctx", scatter_dimension=1, tiled=True),
    )
    attention = (
        (accum_mine / totals_mine[..., None])
        .reshape(rows_here, heads_local * HEAD_WIDTH)
        .astype(jnp.bfloat16)
    )
    local_rows = rows_here // ctx_count
    mixed = lax.psum_scatter(
        jnp.dot(attention, w_out, preferred_element_type=jnp.float32),
        "ctx",
        scatter_dimension=0,
        tiled=True,
    )
    residual = (resid_in.astype(jnp.float32) + mixed).astype(jnp.bfloat16)
    widened = residual.astype(jnp.float32)
    normed = (
        widened * lax.rsqrt(jnp.mean(widened * widened, -1, keepdims=True) + 1e-06) * norm_gain
    ).astype(jnp.bfloat16)
    experts_here = w_gate.shape[0]
    expert_count = expert_place.shape[0]
    device_count = group_count * ctx_count
    capacity = max(2, (3 * local_rows * TOP + 2 * expert_count - 1) // (2 * expert_count))
    flat_ids = expert_ids.reshape(-1)
    one_hot = (flat_ids[:, None] == jnp.arange(expert_count, dtype=jnp.int32)[None, :]).astype(
        jnp.int32
    )
    stored = jnp.sum(one_hot * expert_place[None, :], 1)
    place = jnp.arange(flat_ids.shape[0], dtype=jnp.int32)
    same = (flat_ids[:, None] == flat_ids[None, :]) & (place[None, :] < place[:, None])
    slot_rank = jnp.sum(same.astype(jnp.int32), 1)
    target = (stored * capacity + slot_rank).reshape(local_rows, TOP)
    slot_ids = jnp.arange(expert_count * capacity, dtype=jnp.int32)
    select_mat = jnp.any(slot_ids[:, None, None] == target[None, :, :], 2)
    outgoing = jnp.dot(
        select_mat.astype(jnp.bfloat16), normed, preferred_element_type=jnp.float32
    ).astype(jnp.bfloat16)
    parcels = outgoing.reshape(device_count, experts_here, capacity, D)
    produced = run_experts(
        lax.all_to_all(parcels, ("rows", "ctx"), split_axis=0, concat_axis=0, tiled=True),
        w_gate,
        w_up,
        w_down,
    )
    returned = lax.all_to_all(produced, ("rows", "ctx"), split_axis=0, concat_axis=0, tiled=True)
    returned = returned.reshape(expert_count * capacity, D)
    combine_mat = jnp.sum(
        jnp.where(slot_ids[None, None, :] == target[:, :, None], route_weight[:, :, None], 0.0), 1
    )
    expert_sum = jnp.dot(combine_mat, returned.astype(jnp.float32), precision=lax.Precision.HIGHEST)
    return (widened + expert_sum).astype(jnp.bfloat16)


def solution(mesh):
    return jax.shard_map(
        shards,
        mesh=mesh,
        in_specs=(
            P("rows", None),
            P("ctx", None),
            P("ctx", None),
            P("rows", None),
            P("rows", None),
            P("ctx", None),
            P(("rows", "ctx"), None),
            P(),
            P(("rows", "ctx"), None),
            P(("rows", "ctx"), None),
            P(),
            P(("rows", "ctx"), None, None),
            P(("rows", "ctx"), None, None),
            P(("rows", "ctx"), None, None),
        ),
        out_specs=P(("rows", "ctx"), None),
        check_vma=False,
    )
```

```python
import functools
import math

import jax
import jax.numpy as jnp
from jax import lax
from jax.experimental import pallas as pl
from jax.experimental.pallas import tpu as pltpu
from jax.sharding import PartitionSpec as P

D = 2048
QUERY_HEADS = 32
KEY_HEADS = 4
HEAD_WIDTH = 128
TOP = 8


def run_experts(arrived, w_gate, w_up, w_down):
    gate_proj = jnp.einsum("sjcd,jdf->sjcf", arrived, w_gate, preferred_element_type=jnp.float32)
    up_proj = jnp.einsum("sjcd,jdf->sjcf", arrived, w_up, preferred_element_type=jnp.float32)
    activated = (jax.nn.silu(gate_proj) * up_proj).astype(jnp.bfloat16)
    produced = jnp.einsum("sjcf,jfd->sjcd", activated, w_down, preferred_element_type=jnp.float32)
    return produced.astype(jnp.bfloat16)


def attend_kernel(
    peers,
    local_rows,
    q_ref,
    k_ref,
    v_ref,
    fresh_k_ref,
    fresh_v_ref,
    w_ref,
    resid_ref,
    gain_ref,
    residual_ref,
    normed_ref,
    part_out,
    part_in,
    stat_out,
    stat_in,
    attn,
    mixed_out,
    mixed_in,
    part_sems,
    stat_sems,
    mixed_sems,
):
    me = lax.axis_index("ctx")
    rows_here = q_ref.shape[0]
    heads = QUERY_HEADS // peers
    wide = heads * HEAD_WIDTH
    group = QUERY_HEADS // KEY_HEADS
    scale = 1.0 / math.sqrt(HEAD_WIDTH)

    def peer(step):
        return lax.rem(me + step, peers)

    def lanes(index, width):
        return pl.ds(pl.multiple_of(index * width, width), width)

    def remote(out, into, sems, there, slot):
        return pltpu.make_async_remote_copy(
            src_ref=out.at[there],
            dst_ref=into.at[slot],
            send_sem=sems.at[0, there],
            recv_sem=sems.at[1, slot],
            device_id={"ctx": there},
            device_id_type=pl.DeviceIdType.MESH,
        )

    barrier = pltpu.get_barrier_semaphore()
    for step in range(1, peers):
        pl.semaphore_signal(
            barrier, inc=1, device_id={"ctx": peer(step)}, device_id_type=pl.DeviceIdType.MESH
        )
    pl.semaphore_wait(barrier, peers - 1)

    def partial(owner):
        q_all = q_ref[:, lanes(owner, wide)]
        stacked = jnp.concatenate(
            [q_all[:, h * HEAD_WIDTH : (h + 1) * HEAD_WIDTH] for h in range(heads)], 0
        )
        key_head = (owner * heads) // group
        keys = k_ref[:, lanes(key_head, HEAD_WIDTH)]
        values = v_ref[:, lanes(key_head, HEAD_WIDTH)]
        scores = lax.dot_general(
            keys, stacked, (((1,), (1,)), ((), ())), preferred_element_type=jnp.float32
        )
        top = jnp.max(scores, 0, keepdims=True)
        weights = jnp.exp((scores - top) * scale)
        total = jnp.sum(weights, 0, keepdims=True)
        accum = lax.dot_general(
            values,
            weights.astype(jnp.bfloat16),
            (((0,), (0,)), ((), ())),
            preferred_element_type=jnp.float32,
        )
        place = lax.broadcasted_iota(jnp.int32, (8, top.shape[1]), 0)
        return accum.astype(jnp.bfloat16), jnp.where(place == 0, top * scale, total)

    @pl.loop(1, peers)
    def _(step):
        there = peer(step)
        accum, stats = partial(there)
        part_out[there] = accum
        stat_out[there] = stats
        remote(part_out, part_in, part_sems, there, me).start()
        remote(stat_out, stat_in, stat_sems, there, me).start()

    accum, stats = partial(me)
    part_in[me] = accum
    stat_in[me] = stats

    q_mine = q_ref[:, lanes(me, wide)].astype(jnp.float32)
    key_head = (me * heads) // group
    fresh_k = fresh_k_ref[:, lanes(key_head, HEAD_WIDTH)].astype(jnp.float32)
    fresh_v = fresh_v_ref[:, lanes(key_head, HEAD_WIDTH)].astype(jnp.float32).T
    own = jnp.concatenate(
        [
            jnp.sum((q_mine[:, h * HEAD_WIDTH : (h + 1) * HEAD_WIDTH] * fresh_k).T, 0, keepdims=True)
            for h in range(heads)
        ],
        1,
    ) * scale

    @pl.loop(1, peers)
    def _(step):
        there = peer(step)
        for out, into, sems in ((part_out, part_in, part_sems), (stat_out, stat_in, stat_sems)):
            remote(out, into, sems, there, there).wait_recv()
            remote(out, into, sems, there, me).wait_send()

    top = own
    for c in range(peers):
        top = jnp.maximum(top, stat_in[c, 0:1, :])
    own_weight = jnp.exp(own - top)
    total = own_weight
    numer = jnp.concatenate([fresh_v] * heads, 1) * own_weight
    for c in range(peers):
        factor = jnp.exp(stat_in[c, 0:1, :] - top)
        total = total + stat_in[c, 1:2, :] * factor
        numer = numer + part_in[c].astype(jnp.float32) * factor
    merged = numer / total
    for h in range(heads):
        attn[:, h * HEAD_WIDTH : (h + 1) * HEAD_WIDTH] = merged[
            :, h * rows_here : (h + 1) * rows_here
        ].T.astype(jnp.bfloat16)

    columns = min(512, D)
    for t in range(D // columns):
        cols = slice(t * columns, (t + 1) * columns)
        product = jnp.dot(attn[...], w_ref[:, cols], preferred_element_type=jnp.float32)
        for c in range(peers):
            mixed_out[c, 0:local_rows, cols] = product[
                c * local_rows : (c + 1) * local_rows
            ].astype(jnp.bfloat16)

    @pl.loop(1, peers)
    def _(step):
        remote(mixed_out, mixed_in, mixed_sems, peer(step), me).start()

    mixed_in[me] = mixed_out[me]

    @pl.loop(1, peers)
    def _(step):
        there = peer(step)
        remote(mixed_out, mixed_in, mixed_sems, there, there).wait_recv()
        remote(mixed_out, mixed_in, mixed_sems, there, me).wait_send()

    mixed = resid_ref[...].astype(jnp.float32)
    for c in range(peers):
        mixed = mixed + mixed_in[c, 0:local_rows, :].astype(jnp.float32)
    residual = mixed.astype(jnp.bfloat16)
    widened = residual.astype(jnp.float32)
    residual_ref[...] = residual
    normed_ref[...] = (
        widened
        * lax.rsqrt(jnp.mean(widened * widened, -1, keepdims=True) + 1e-06)
        * gain_ref[...]
    ).astype(jnp.bfloat16)


def attend(queries, keys, values, fresh_keys, fresh_values, w_out, resid_in, norm_gain):
    peers = lax.axis_size("ctx")
    rows_here = queries.shape[0]
    local_rows = rows_here // peers
    lanes = QUERY_HEADS // peers * HEAD_WIDTH
    stat_lanes = QUERY_HEADS // peers * rows_here
    block = (peers, -(-local_rows // 16) * 16, D)
    shape = jax.ShapeDtypeStruct((local_rows, D), jnp.bfloat16)
    vmem = pl.BlockSpec(memory_space=pltpu.VMEM)
    return pl.pallas_call(
        functools.partial(attend_kernel, peers, local_rows),
        out_shape=(shape, shape),
        in_specs=[vmem] * 8,
        out_specs=(vmem, vmem),
        scratch_shapes=[
            pltpu.VMEM((peers, HEAD_WIDTH, stat_lanes), jnp.bfloat16),
            pltpu.VMEM((peers, HEAD_WIDTH, stat_lanes), jnp.bfloat16),
            pltpu.VMEM((peers, 8, stat_lanes), jnp.float32),
            pltpu.VMEM((peers, 8, stat_lanes), jnp.float32),
            pltpu.VMEM((rows_here, lanes), jnp.bfloat16),
            pltpu.VMEM(block, jnp.bfloat16),
            pltpu.VMEM(block, jnp.bfloat16),
            pltpu.SemaphoreType.DMA((2, peers)),
            pltpu.SemaphoreType.DMA((2, peers)),
            pltpu.SemaphoreType.DMA((2, peers)),
        ],
        compiler_params=pltpu.CompilerParams(
            collective_id=0, has_side_effects=True, vmem_limit_bytes=40 * 2**20
        ),
    )(
        queries,
        keys,
        values,
        fresh_keys,
        fresh_values,
        w_out,
        resid_in,
        norm_gain.reshape(1, D),
    )


def shards(
    queries,
    prefix_key_cache,
    prefix_value_cache,
    fresh_token_key,
    fresh_token_value,
    w_out,
    resid_in,
    norm_gain,
    expert_ids,
    route_weight,
    expert_place,
    w_gate,
    w_up,
    w_down,
):
    rows_here = queries.shape[0]
    ctx_count = lax.axis_size("ctx")
    group_count = lax.axis_size("rows")
    local_rows = rows_here // ctx_count
    residual, normed = attend(
        queries,
        prefix_key_cache,
        prefix_value_cache,
        fresh_token_key,
        fresh_token_value,
        w_out,
        resid_in,
        norm_gain,
    )
    widened = residual.astype(jnp.float32)
    experts_here = w_gate.shape[0]
    expert_count = expert_place.shape[0]
    device_count = group_count * ctx_count
    capacity = max(2, (3 * local_rows * TOP + 2 * expert_count - 1) // (2 * expert_count))
    flat_ids = expert_ids.reshape(-1)
    one_hot = (flat_ids[:, None] == jnp.arange(expert_count, dtype=jnp.int32)[None, :]).astype(
        jnp.int32
    )
    stored = jnp.sum(one_hot * expert_place[None, :], 1)
    place = jnp.arange(flat_ids.shape[0], dtype=jnp.int32)
    same = (flat_ids[:, None] == flat_ids[None, :]) & (place[None, :] < place[:, None])
    slot_rank = jnp.sum(same.astype(jnp.int32), 1)
    target = (stored * capacity + slot_rank).reshape(local_rows, TOP)
    slot_ids = jnp.arange(expert_count * capacity, dtype=jnp.int32)
    select_mat = jnp.any(slot_ids[:, None, None] == target[None, :, :], 2)
    outgoing = jnp.dot(
        select_mat.astype(jnp.bfloat16), normed, preferred_element_type=jnp.float32
    ).astype(jnp.bfloat16)
    parcels = outgoing.reshape(device_count, experts_here, capacity, D)
    produced = run_experts(
        lax.all_to_all(parcels, ("rows", "ctx"), split_axis=0, concat_axis=0, tiled=True),
        w_gate,
        w_up,
        w_down,
    )
    returned = lax.all_to_all(produced, ("rows", "ctx"), split_axis=0, concat_axis=0, tiled=True)
    returned = returned.reshape(expert_count * capacity, D)
    combine_mat = jnp.sum(
        jnp.where(slot_ids[None, None, :] == target[:, :, None], route_weight[:, :, None], 0.0), 1
    )
    expert_sum = jnp.dot(combine_mat, returned.astype(jnp.float32), precision=lax.Precision.HIGHEST)
    return (widened + expert_sum).astype(jnp.bfloat16)


def solution(mesh):
    return jax.shard_map(
        shards,
        mesh=mesh,
        in_specs=(
            P("rows", None),
            P("ctx", None),
            P("ctx", None),
            P("rows", None),
            P("rows", None),
            P("ctx", None),
            P(("rows", "ctx"), None),
            P(),
            P(("rows", "ctx"), None),
            P(("rows", "ctx"), None),
            P(),
            P(("rows", "ctx"), None, None),
            P(("rows", "ctx"), None, None),
            P(("rows", "ctx"), None, None),
        ),
        out_specs=P(("rows", "ctx"), None),
        check_vma=False,
    )
```
